32 devices in a mesh: groups: 2 (over y), blocks: 8 (over z, x), span: 2 (over core).
Axes of the slice: x: 2, y: 2, z: 4, core: 2. Of those that a mesh axis runs over, the one named last changes fastest.
Arguments:
- state: float32 [9, 6, 16, 2, 8, 512], P(None, None, ('groups', 'blocks'), None, None, 'span'), parts along dimension 2, may hold values from -4 to 4
- source: float32 [9, 6, 16, 2, 8, 512], P(None, None, ('groups', 'blocks'), None, None, 'span'), parts along dimension 2, may hold values from -6 to 6
- block_matrix: float32 [6, 6, 16, 2, 8, 512], P(None, None, ('groups', 'blocks'), None, None, 'span'), parts along dimension 2, may hold values from -1 to 16, as said below
- phase_index: int32 [8], P('groups'), parts along dimension 0, may hold values from 1 to 63
- face_pair: int32 [2048], replicated, may hold values from 0 to 2047, each once
Outputs:
- new_state: float32 [9, 6, 16, 2, 8, 512], P(None, None, ('groups', 'blocks'), None, None, 'span'), parts along dimension 2
- residual: float32 [9, 6, 16, 2, 8, 512], P(None, None, ('groups', 'blocks'), None, None, 'span'), parts along dimension 2
The draws below stay inside these ranges and needn't reach their ends.
There are 2 independent parts, one for each index of `groups`. The reference program is written for one: setup_inputs(seed, part) draws one part's arguments, and reference() takes and returns one part's arrays. A program takes and returns all parts, laid end to end along the dimension named above; an argument that names none is the same for every part. Nothing has to cross between parts.
Inputs may be any that keep to these rules, and one draw needn't show every extreme that they name: `block_matrix`: entries whose two variable indices are equal lie between 10 and 16; all others between -1 and 1.
All inputs are finite; a program needn't handle non-finite values.
Results may differ from the reference program's by a relative error of at most 0.0001.
Values sent between devices are 32-bit elements; how exact they have to be, the bound alone decides.
No kernel may reach another device: no remote copies, remote signals or barrier semaphores. Data moves between devices by JAX's collectives and lax.ppermute only.
A program may use at most 64 MiB of HBM per device.

```python
import math
import jax
import jax.numpy as jnp
from jax import lax

NI = 9
NV = 6
NPASS = 64
AXB = 2
NSWEEP = 3
CT = 2
CA = 8
CS = 256
NH = 4
NBLK = 8
NTH = 8
NAX = 16
NS = 512
FACE = 2048
N_SPAN = 2


def draw_block_matrix(key, part):
    key = jax.random.fold_in(key, 5)
    key_off, key_diag = jax.random.split(key)
    full_shape = (NV, NV, NBLK, CT, CA, NS)
    off_entries = jax.random.uniform(key_off, full_shape, jnp.float32, -1.0, 1.0)
    diag_entries = jax.random.uniform(key_diag, full_shape, jnp.float32, 10.0, 16.0)
    picker = (jnp.arange(NV)[:, None] == jnp.arange(NV)[None, :]).reshape(NV, NV, 1, 1, 1, 1)
    return jnp.where(picker, diag_entries, off_entries)


def touch_ends(entries, key, smallest, high):
    dims = entries.shape
    index_at = [jax.random.randint(jax.random.fold_in(key, axis), (), 0, dims[axis]) for axis in range(len(dims))]
    entries = entries.at[tuple(index_at)].set(smallest)
    longest = dims.index(max(dims))
    index_at[longest] = (index_at[longest] + 1) % dims[longest]
    return entries.at[tuple(index_at)].set(high)


def shard_levels(rng, shape, shards, low, largest):
    loudness = 1.0
    for dim, shards_of in shards:
        draws = jax.random.uniform(jax.random.fold_in(jax.random.fold_in(rng, 6), dim), (shards_of,), jnp.float32, low / len(shards), largest / len(shards))
        loudness = loudness * jnp.repeat(jnp.exp(draws), shape[dim] // shards_of).reshape((-1,) + (1,) * (len(shape) - 1 - dim))
    return loudness


def gaussian(rng, shape, spread, most, cuts=(), kind=jnp.bfloat16):
    loudness = shard_levels(rng, shape, cuts, -0.22, 0.18) if cuts else 1.0
    drawn = jax.random.normal(rng, shape, jnp.float32) * spread * loudness
    return jnp.minimum(jnp.maximum(drawn, -most), most).astype(kind)


def setup_inputs(seed: int = 0, part: int = 0) -> dict:
    keys = jax.random.split(jax.random.key(seed), 6)
    own_keys = jax.random.split(jax.random.fold_in(keys[5], part), 6)
    state = gaussian(own_keys[0], (NI, NV, NBLK, CT, CA, NS), 0.3, 4.0, ((2, 8), (5, 2)), jnp.float32)
    source = gaussian(own_keys[1], (NI, NV, NBLK, CT, CA, NS), 1.0, 6.0, ((2, 8), (5, 2)), jnp.float32)
    block_matrix = draw_block_matrix(jax.random.fold_in(jax.random.fold_in(keys[5], part), 71), part)
    phase_index = touch_ends(jax.random.randint(own_keys[3], (NH,), 1, NPASS), jax.random.fold_in(own_keys[3], 1), 1, NPASS - 1).astype(jnp.int32)
    face_pair = jax.random.permutation(keys[4], FACE).astype(jnp.int32)
    return {"state": state, "source": source, "block_matrix": block_matrix, "phase_index": phase_index, "face_pair": face_pair}


def instance_tables(phase_index, instances):
    harmonics = (instances - 1) // 2
    angles = 2.0 * math.pi * jnp.arange(instances, dtype=jnp.float32) / instances
    spacing = angles[:, None] - angles[None, :]
    orders = jnp.arange(1, harmonics + 1, dtype=jnp.float32)
    phases = 2.0 * math.pi * phase_index.astype(jnp.float32) / NPASS
    argument = orders[:, None, None] * spacing[None]
    shift_plus = (1.0 + 2.0 * jnp.sum(jnp.cos(argument + phases[:, None, None]), axis=0)) / instances
    shift_minus = (1.0 + 2.0 * jnp.sum(jnp.cos(argument - phases[:, None, None]), axis=0)) / instances
    spectral = -(2.0 / instances) * jnp.sum(orders[:, None, None] * jnp.sin(argument), axis=0)
    return shift_plus, shift_minus, spectral


def mix_instances(matrix, state_now):
    flat_view = state_now.reshape(state_now.shape[0], -1)
    mixed = jnp.dot(matrix, flat_view, precision=lax.Precision.HIGHEST, preferred_element_type=jnp.float32)
    return mixed.reshape(state_now.shape)


def apply_block(matrix, state_now):
    accum_term = matrix[None, :, 0] * state_now[:, None, 0]
    for column in range(1, state_now.shape[1]):
        accum_term = accum_term + matrix[None, :, column] * state_now[:, None, column]
    return accum_term


def split_block(matrix):
    variables = matrix.shape[0]
    picker = (jnp.arange(variables)[:, None] == jnp.arange(variables)[None, :])
    picker = picker.reshape((variables, variables) + (1,) * (matrix.ndim - 2))
    offblock = jnp.where(picker, jnp.zeros_like(matrix), matrix)
    diagonal = jnp.stack([matrix[variable, variable] for variable in range(variables)])
    return diagonal, offblock


def point_solve(residual, diagonal, offblock, spectral):
    result = residual / diagonal[None]
    for sweep_index in range(NSWEEP):
        result = (residual - apply_block(offblock, result) - mix_instances(spectral, result)) / diagonal[None]
    return result


def neighbour_sum(state_now, ghosts):
    lower_circ, upper_circ, lower_axial, upper_axial, lower_span, upper_span = ghosts
    near_sum = jnp.concatenate([lower_circ[:, :, None], state_now[:, :, :-1]], axis=2)
    near_sum = near_sum + jnp.concatenate([state_now[:, :, 1:], upper_circ[:, :, None]], axis=2)
    near_sum = near_sum + jnp.concatenate([lower_axial[:, :, :, None], state_now[:, :, :, :-1]], axis=3)
    near_sum = near_sum + jnp.concatenate([state_now[:, :, :, 1:], upper_axial[:, :, :, None]], axis=3)
    near_sum = near_sum + jnp.concatenate([lower_span[..., None], state_now[..., :-1]], axis=4)
    near_sum = near_sum + jnp.concatenate([state_now[..., 1:], upper_span[..., None]], axis=4)
    return near_sum


def to_grid(blocked):
    lead_dim, next_dim = blocked.shape[0], blocked.shape[1]
    shaped = blocked.reshape(lead_dim, next_dim, NBLK // AXB, AXB, CT, CA, NS)
    return shaped.transpose(0, 1, 2, 4, 3, 5, 6).reshape(lead_dim, next_dim, NTH, NAX, NS)


def from_grid(gridded):
    lead_dim, next_dim = gridded.shape[0], gridded.shape[1]
    shaped = gridded.reshape(lead_dim, next_dim, NBLK // AXB, CT, AXB, CA, NS)
    return shaped.transpose(0, 1, 2, 4, 3, 5, 6).reshape(lead_dim, next_dim, NBLK, CT, CA, NS)


def pair_face(face_layer, pairing):
    lead_dim, next_dim = face_layer.shape[0], face_layer.shape[1]
    shaped = face_layer.reshape(lead_dim, next_dim, AXB, CA, N_SPAN, CS).transpose(0, 1, 2, 4, 3, 5)
    shaped = shaped.reshape(lead_dim, next_dim, AXB * N_SPAN, CA * CS)
    picked = jnp.take(shaped, pairing, axis=3)
    picked = picked.reshape(lead_dim, next_dim, AXB, N_SPAN, CA, CS).transpose(0, 1, 2, 4, 3, 5)
    return picked.reshape(lead_dim, next_dim, NAX, NS)


def reference(state, source, block_matrix, phase_index, face_pair):
    shift_plus, shift_minus, spectral = instance_tables(phase_index, NI)
    state_now = to_grid(state)
    forcing = to_grid(source)
    matrix = to_grid(block_matrix)
    inverse = jnp.zeros_like(face_pair).at[face_pair].set(jnp.arange(FACE, dtype=jnp.int32))
    lower_ghost = mix_instances(shift_minus, pair_face(state_now[:, :, -1], face_pair))
    upper_ghost = mix_instances(shift_plus, pair_face(state_now[:, :, 0], inverse))
    zero_axial = jnp.zeros((NI, NV, NTH, NS), jnp.float32)
    zero_span = jnp.zeros((NI, NV, NTH, NAX), jnp.float32)
    near_sum = neighbour_sum(state_now, (lower_ghost, upper_ghost, zero_axial, zero_axial, zero_span, zero_span))
    local_term = apply_block(matrix, state_now)
    time_term = mix_instances(spectral, state_now)
    residual = forcing - (local_term - near_sum + time_term)
    diagonal, offblock = split_block(matrix)
    update = point_solve(residual, diagonal, offblock, spectral)
    return from_grid(state_now + update), from_grid(residual)
```

```python
import functools
import math

import jax
import jax.numpy as jnp
from jax import lax
from jax.experimental import pallas as pl
from jax.experimental.pallas import tpu as pltpu
from jax.sharding import PartitionSpec as P

NPASS = 64
AXB = 2
NSWEEP = 3
LANES = 128
VMEM_LIMIT = 48 * 1024 * 1024


def rotations(phase_index, instances):
    harmonics = (instances - 1) // 2
    spacing = 2.0 * math.pi * jnp.arange(instances, dtype=jnp.float32) / instances
    orders = jnp.arange(1, harmonics + 1, dtype=jnp.float32)
    phases = 2.0 * math.pi * phase_index.astype(jnp.float32) / NPASS
    argument = orders[:, None] * spacing[None]
    plus = (1.0 + 2.0 * jnp.sum(jnp.cos(argument + phases[:, None]), axis=0)) / instances
    minus = (1.0 + 2.0 * jnp.sum(jnp.cos(argument - phases[:, None]), axis=0)) / instances
    return plus, minus


def spectral_weights(instances):
    harmonics = (instances - 1) // 2
    return [
        -(2.0 / instances)
        * sum(k * math.sin(2.0 * math.pi * k * d / instances) for k in range(1, harmonics + 1))
        for d in range(1, harmonics + 1)
    ]


def spectral_mix(values):
    count = len(values)
    mixed = []
    for n in range(count):
        total = None
        for d, weight in enumerate(spectral_weights(count), 1):
            term = weight * (values[(n - d) % count] - values[(n + d) % count])
            total = term if total is None else total + term
        mixed.append(total)
    return mixed


def take_lanes(tile, index):
    return jnp.take_along_axis(tile, index, axis=1, mode="promise_in_bounds")


def inverse_pairing(pairing):
    axial, span = pairing.shape
    tiles = span // LANES
    rows = axial * tiles
    row = lax.broadcasted_iota(jnp.int32, (rows, span), 0)
    wanted_row = (row % axial) * tiles + row // axial
    place = lax.broadcasted_iota(jnp.int32, (rows, span), 1)
    lane = lax.broadcasted_iota(jnp.int32, (LANES, span), 0)
    total = jnp.zeros((2 * rows, LANES), jnp.float32)
    for a in range(axial):
        target = pairing[a : a + 1]
        hit = wanted_row == target // LANES
        origin = place + a * span
        high = jnp.where(hit, origin // LANES, 0)
        low = jnp.where(hit, origin % LANES, 0)
        left = jnp.concatenate([high, low], axis=0).astype(jnp.float32).astype(jnp.bfloat16)
        right = (lane == target % LANES).astype(jnp.float32).astype(jnp.bfloat16)
        total = total + lax.dot_general(
            left, right, (((1,), (1,)), ((), ())), preferred_element_type=jnp.float32
        )
    cells = (total[:rows] * LANES + total[rows:]).astype(jnp.int32)
    return [cells[t * axial : (t + 1) * axial] for t in range(tiles)]


def far_face_kernel(place, turn, pairing, layer, *outs_and_scratch):
    *outs, index = outs_and_scratch
    instances, variables, _, _, axial, span = layer.shape
    tiles = span // LANES

    @pl.when(place[2] == 1)
    def _():
        for t, cells in enumerate(inverse_pairing(pairing[...])):
            index[t] = cells

    @pl.when(place[3] == 1)
    def _():
        for t in range(tiles):
            index[t] = pairing[:, t * LANES : (t + 1) * LANES]

    @pl.when(place[2] + place[3] == 0)
    def _():
        for t, out in enumerate(outs):
            out[...] = layer[:, :, 0, 0, :, t * LANES : (t + 1) * LANES]

    @pl.when(place[2] + place[3] > 0)
    def _():
        for t, out in enumerate(outs):
            lane = index[t] % LANES
            row = index[t] // LANES

            @pl.loop(0, variables)
            def _(v):
                picked = [jnp.zeros((axial, LANES), jnp.float32)] * instances
                for a in range(axial):
                    for s in range(tiles):
                        hit = row == a * tiles + s
                        for i in range(instances):
                            line = layer[i, v, 0, 0, a : a + 1, s * LANES : (s + 1) * LANES]
                            line = jnp.broadcast_to(line, (axial, LANES))
                            picked[i] = jnp.where(hit, take_lanes(line, lane), picked[i])
                for n in range(instances):
                    total = turn[n] * picked[0]
                    for m in range(1, instances):
                        total = total + turn[(n - m) % instances] * picked[m]
                    out[n, v] = total


def faces_kernel(place, state, axial_face, span_face):
    instances, variables, _, circ, axial, span = state.shape
    edge = jnp.where(place[4] == 0, axial - 1, 0)
    last = (place[5] == 0).astype(jnp.int32)
    lane = lax.broadcasted_iota(jnp.int32, (axial, LANES), 1)
    edge_lane = jnp.full((axial, LANES), last * (LANES - 1), jnp.int32)
    start = pl.multiple_of(last * (span - LANES), LANES)
    columns = jnp.zeros((axial, LANES), jnp.float32)
    for c in range(circ):
        for i in range(instances):
            for v in range(variables):
                k = (c * instances + i) * variables + v
                axial_face[k : k + 1] = state[i, v, 0, c, pl.ds(edge, 1), :]
                tile = take_lanes(state[i, v, 0, c, :, pl.ds(start, LANES)], edge_lane)
                columns = jnp.where(lane == k, tile, columns)
    span_face[...] = columns


def solve_tile(residual, matrix, count):
    instances, variables = count
    scale = [1.0 / matrix(v, v) for v in range(variables)]
    first = [[residual[i][v] * scale[v] for v in range(variables)] for i in range(instances)]
    update = first
    for _ in range(NSWEEP):
        later = [[None] * variables for _ in range(instances)]
        for v in range(variables):
            total = spectral_mix([update[i][v] for i in range(instances)])
            for w in range(variables):
                if w != v:
                    entry = matrix(v, w)
                    for i in range(instances):
                        total[i] = total[i] + entry * update[i][w]
            for i in range(instances):
                later[i][v] = first[i][v] - scale[v] * total[i]
        update = later
    return update


def near_kernel(place, state, source, matrix, ghost, axial_ghost, span_ghost, residual, updated):
    instances, variables, _, circ, axial, span = state.shape
    row = lax.broadcasted_iota(jnp.int32, (axial, span), 0)
    column = lax.broadcasted_iota(jnp.int32, (axial, span), 1)
    axial_row = jnp.where(place[4] == 0, axial - 1, 0)
    span_column = jnp.where(place[5] == 0, span - 1, 0)
    columns = span_ghost[...]

    @pl.loop(0, circ * variables)
    def _(step):
        c = step // variables
        v = step % variables
        near_layer = place[0] == c
        own = [state[i, v, 0, c] for i in range(instances)]
        timed = spectral_mix(own)
        for i in range(instances):
            k = (c * instances + i) * variables + v
            near = state[i, v, 0, 1 - c] + jnp.where(near_layer, ghost[i, v], 0.0)
            near = near + jnp.where(row == 0, 0.0, pltpu.roll(own[i], 1, 0))
            near = near + jnp.where(row == axial - 1, 0.0, pltpu.roll(own[i], axial - 1, 0))
            near = near + jnp.where(row == axial_row, axial_ghost[pl.ds(k, 1), :], 0.0)
            near = near + jnp.where(column == 0, 0.0, pltpu.roll(own[i], 1, 1))
            near = near + jnp.where(column == span - 1, 0.0, pltpu.roll(own[i], span - 1, 1))
            edge = take_lanes(columns, jnp.full((axial, LANES), k, jnp.int32))
            edge = jnp.concatenate([edge] * (span // LANES), axis=1)
            near = near + jnp.where(column == span_column, edge, 0.0)
            local = matrix[v, 0, 0, c] * state[i, 0, 0, c]
            for w in range(1, variables):
                local = local + matrix[v, w, 0, c] * state[i, w, 0, c]
            residual[i, v, 0, c] = source[i, v, 0, c] - (local - near + timed[i])

    c = place[0]

    @pl.loop(0, span // LANES)
    def _(t):
        lanes = pl.ds(pl.multiple_of(t * LANES, LANES), LANES)
        right = [
            [residual[i, v, 0, c, :, lanes] for v in range(variables)] for i in range(instances)
        ]
        update = solve_tile(
            right, lambda v, w: matrix[v, w, 0, c, :, lanes], (instances, variables)
        )
        for i in range(instances):
            for v in range(variables):
                updated[i, v, 0, c, :, lanes] = state[i, v, 0, c, :, lanes] + update[i][v]


def far_kernel(place, partial, _, state, matrix, ghost, residual, updated):
    instances, variables = ghost.shape[:2]
    right = []
    for i in range(instances):
        right.append([])
        for v in range(variables):
            value = partial[i, v, 0, 0] + ghost[i, v]
            residual[i, v, 0, 0] = value
            right[i].append(value)
    update = solve_tile(right, lambda v, w: matrix[v, w, 0, 0], (instances, variables))
    for i in range(instances):
        for v in range(variables):
            updated[i, v, 0, 0] = state[i, v, 0, 0] + update[i][v]


def whole(shape, *, space=pltpu.VMEM):
    zeros = (0,) * len(shape)
    return pl.BlockSpec(shape, lambda step, place: zeros, memory_space=space)


def call(kernel, name, operands, in_specs, outs, out_specs, scratch=(), aliases=None):
    return pl.pallas_call(
        kernel,
        name=name,
        grid_spec=pltpu.PrefetchScalarGridSpec(
            num_scalar_prefetch=1,
            grid=(1,),
            in_specs=in_specs,
            out_specs=out_specs,
            scratch_shapes=scratch,
        ),
        out_shape=outs,
        input_output_aliases=aliases or {},
        compiler_params=pltpu.CompilerParams(vmem_limit_bytes=VMEM_LIMIT),
    )(*operands)


def shards(state, source, block_matrix, phase_index, face_pair):
    instances, variables, _, circ, axial, span = state.shape
    tiles = span // LANES
    blocks = lax.axis_size("blocks")
    rings = blocks // AXB
    position = lax.axis_index("blocks")
    circ_place = position // AXB
    even = circ_place % 2 == 0
    near_layer = jnp.where(even, circ - 1, 0)
    far_layer = jnp.where(even, 0, circ - 1)
    at_first = circ_place == 0
    at_last = circ_place == rings - 1
    place = jnp.stack(
        [
            near_layer,
            far_layer,
            at_first,
            at_last,
            position % AXB,
            lax.axis_index("span"),
        ]
    ).astype(jnp.int32)

    def ring_partner(block, first):
        hop = 1 if block // AXB % 2 == first else -1
        return (block // AXB + hop) % rings * AXB + block % AXB

    near_route = [(b, ring_partner(b, 0)) for b in range(blocks)]
    far_route = [(b, ring_partner(b, 1)) for b in range(blocks)]
    axial_route = [(b, b ^ 1) for b in range(blocks)]

    near_face = lax.dynamic_slice_in_dim(state, near_layer, 1, 3)[:, :, 0, 0]
    near_ghost = lax.ppermute(near_face, "blocks", near_route)

    plus, minus = rotations(phase_index, instances)
    turn = jnp.where(at_first, plus, minus)
    pairing = face_pair.reshape(axial, span)
    layer_shape = (instances, variables, 1, 1, axial, span)
    chunk = jax.ShapeDtypeStruct((instances, variables, axial, LANES), jnp.float32)
    far_faces = call(
        far_face_kernel,
        "far_face",
        (place, turn, pairing, state),
        [
            pl.BlockSpec(memory_space=pltpu.SMEM),
            whole((axial, span)),
            pl.BlockSpec(layer_shape, lambda step, place: (0, 0, 0, place[1], 0, 0)),
        ],
        [chunk] * tiles,
        [whole(chunk.shape)] * tiles,
        [pltpu.VMEM((tiles, axial, LANES), jnp.int32)],
    )
    far_ghosts = [lax.ppermute(face, "blocks", far_route) for face in far_faces]

    faces = circ * instances * variables
    axial_face, span_face = call(
        faces_kernel,
        "faces",
        (place, state),
        [whole(state.shape)],
        [
            jax.ShapeDtypeStruct((faces, span), jnp.float32),
            jax.ShapeDtypeStruct((axial, LANES), jnp.float32),
        ],
        [whole((faces, span)), whole((axial, LANES))],
    )
    axial_ghost = lax.ppermute(axial_face, "blocks", axial_route)
    span_ghost = lax.ppermute(span_face, "span", [(0, 1), (1, 0)])

    out = jax.ShapeDtypeStruct(state.shape, jnp.float32)
    residual, updated = call(
        near_kernel,
        "near",
        (place, state, source, block_matrix, near_ghost, axial_ghost, span_ghost),
        [
            whole(state.shape),
            whole(source.shape),
            whole(block_matrix.shape),
            whole(near_ghost.shape),
            whole(axial_ghost.shape),
            whole(span_ghost.shape),
        ],
        [out, out],
        [whole(out.shape), whole(out.shape)],
    )

    for t, ghost in enumerate(far_ghosts):
        def part(lead):
            return pl.BlockSpec(
                (lead, variables, 1, 1, axial, LANES),
                lambda step, place: (0, 0, 0, place[1], 0, t),
            )

        residual, updated = call(
            far_kernel,
            "far",
            (place, residual, updated, state, block_matrix, ghost),
            [
                part(instances),
                pl.BlockSpec(memory_space=pl.ANY),
                part(instances),
                part(variables),
                whole(ghost.shape),
            ],
            [out, out],
            [part(instances), part(instances)],
            aliases={1: 0, 2: 1},
        )
    return updated, residual


def solution(mesh):
    placed = P(None, None, ("groups", "blocks"), None, None, "span")
    return jax.shard_map(
        shards,
        mesh=mesh,
        in_specs=(placed, placed, placed, P("groups"), P()),
        out_specs=(placed, placed),
        check_vma=False,
    )
```

```python
import functools
import math

import jax
import jax.numpy as jnp
from jax import lax
from jax.experimental import pallas as pl
from jax.experimental.pallas import tpu as pltpu
from jax.sharding import PartitionSpec as P

NPASS = 64
AXB = 2
NSWEEP = 3
LANES = 128
VMEM_LIMIT = 48 * 1024 * 1024


def rotations(phase_index, instances):
    harmonics = (instances - 1) // 2
    spacing = 2.0 * math.pi * jnp.arange(instances, dtype=jnp.float32) / instances
    orders = jnp.arange(1, harmonics + 1, dtype=jnp.float32)
    phases = 2.0 * math.pi * phase_index.astype(jnp.float32) / NPASS
    argument = orders[:, None] * spacing[None]
    plus = (1.0 + 2.0 * jnp.sum(jnp.cos(argument + phases[:, None]), axis=0)) / instances
    minus = (1.0 + 2.0 * jnp.sum(jnp.cos(argument - phases[:, None]), axis=0)) / instances
    return plus, minus


def spectral_weights(instances):
    harmonics = (instances - 1) // 2
    return [
        -(2.0 / instances)
        * sum(k * math.sin(2.0 * math.pi * k * d / instances) for k in range(1, harmonics + 1))
        for d in range(1, harmonics + 1)
    ]


def spectral_mix(values):
    count = len(values)
    mixed = []
    for n in range(count):
        total = None
        for d, weight in enumerate(spectral_weights(count), 1):
            term = weight * (values[(n - d) % count] - values[(n + d) % count])
            total = term if total is None else total + term
        mixed.append(total)
    return mixed


def take_lanes(tile, index):
    return jnp.take_along_axis(tile, index, axis=1, mode="promise_in_bounds")


def inverse_pairing(pairing):
    axial, span = pairing.shape
    tiles = span // LANES
    rows = axial * tiles
    row = lax.broadcasted_iota(jnp.int32, (rows, span), 0)
    wanted_row = (row % axial) * tiles + row // axial
    place = lax.broadcasted_iota(jnp.int32, (rows, span), 1)
    lane = lax.broadcasted_iota(jnp.int32, (LANES, span), 0)
    total = jnp.zeros((2 * rows, LANES), jnp.float32)
    for a in range(axial):
        target = pairing[a : a + 1]
        hit = wanted_row == target // LANES
        origin = place + a * span
        high = jnp.where(hit, origin // LANES, 0)
        low = jnp.where(hit, origin % LANES, 0)
        left = jnp.concatenate([high, low], axis=0).astype(jnp.float32).astype(jnp.bfloat16)
        right = (lane == target % LANES).astype(jnp.float32).astype(jnp.bfloat16)
        total = total + lax.dot_general(
            left, right, (((1,), (1,)), ((), ())), preferred_element_type=jnp.float32
        )
    cells = (total[:rows] * LANES + total[rows:]).astype(jnp.int32)
    return [cells[t * axial : (t + 1) * axial] for t in range(tiles)]


def places():
    rings = lax.axis_size("blocks") // AXB
    position = lax.axis_index("blocks")
    ring = position // AXB
    near = 1 - ring % 2
    return near, 1 - near, ring == 0, ring == rings - 1, position % AXB, lax.axis_index("span")


def split_kernel(state, far_face, near_face, sems):
    near, far = places()[:2]
    copies = [
        pltpu.make_async_copy(state.at[:, :, 0, far], far_face, sems.at[0]),
        pltpu.make_async_copy(state.at[:, :, 0, near], near_face, sems.at[1]),
    ]
    for copy in copies:
        copy.start()
    for copy in copies:
        copy.wait()


def paired_kernel(turn, pairing, state, _, *outs_and_scratch):
    *outs, index = outs_and_scratch
    instances, variables, _, _, axial, span = state.shape
    tiles = span // LANES
    _, far, first, last, _, _ = places()

    @pl.when(first)
    def _():
        for t, cells in enumerate(inverse_pairing(pairing[...])):
            index[t] = cells

    @pl.when(last)
    def _():
        for t in range(tiles):
            index[t] = pairing[:, t * LANES : (t + 1) * LANES]

    @pl.when(first | last)
    def _():
        for t, out in enumerate(outs):
            lane = index[t] % LANES
            row = index[t] // LANES

            @pl.loop(0, variables)
            def _(v):
                picked = [jnp.zeros((axial, LANES), jnp.float32)] * instances
                for a in range(axial):
                    for s in range(tiles):
                        hit = row == a * tiles + s
                        for i in range(instances):
                            line = state[i, v, 0, far, a : a + 1, s * LANES : (s + 1) * LANES]
                            line = jnp.broadcast_to(line, (axial, LANES))
                            picked[i] = jnp.where(hit, take_lanes(line, lane), picked[i])
                for n in range(instances):
                    total = turn[n] * picked[0]
                    for m in range(1, instances):
                        total = total + turn[(n - m) % instances] * picked[m]
                    out[n, v] = total


def faces_kernel(state, axial_face, span_face):
    instances, variables, _, circ, axial, span = state.shape
    _, _, _, _, axial_place, span_place = places()
    edge = jnp.where(axial_place == 0, axial - 1, 0)
    last = (span_place == 0).astype(jnp.int32)
    lane = lax.broadcasted_iota(jnp.int32, (axial, LANES), 1)
    edge_lane = jnp.full((axial, LANES), last * (LANES - 1), jnp.int32)
    start = pl.multiple_of(last * (span - LANES), LANES)
    columns = jnp.zeros((axial, LANES), jnp.float32)
    for c in range(circ):
        for i in range(instances):
            for v in range(variables):
                k = (c * instances + i) * variables + v
                axial_face[k : k + 1] = state[i, v, 0, c, pl.ds(edge, 1), :]
                tile = take_lanes(state[i, v, 0, c, :, pl.ds(start, LANES)], edge_lane)
                columns = jnp.where(lane == k, tile, columns)
    span_face[...] = columns


def solve_tile(residual, matrix, count):
    instances, variables = count
    scale = [1.0 / matrix(v, v) for v in range(variables)]
    first = [[residual[i][v] * scale[v] for v in range(variables)] for i in range(instances)]
    update = first
    for _ in range(NSWEEP):
        later = [[None] * variables for _ in range(instances)]
        for v in range(variables):
            total = spectral_mix([update[i][v] for i in range(instances)])
            for w in range(variables):
                if w != v:
                    entry = matrix(v, w)
                    for i in range(instances):
                        total[i] = total[i] + entry * update[i][w]
            for i in range(instances):
                later[i][v] = first[i][v] - scale[v] * total[i]
        update = later
    return update


def base_kernel(state, source, matrix, axial_ghost, span_ghost, partial):
    instances, variables, _, circ, axial, span = state.shape
    _, _, _, _, axial_place, span_place = places()
    row = lax.broadcasted_iota(jnp.int32, (axial, span), 0)
    column = lax.broadcasted_iota(jnp.int32, (axial, span), 1)
    axial_row = jnp.where(axial_place == 0, axial - 1, 0)
    span_column = jnp.where(span_place == 0, span - 1, 0)
    columns = span_ghost[...]

    @pl.loop(0, circ * variables)
    def _(step):
        c = step // variables
        v = step % variables
        own = [state[i, v, 0, c] for i in range(instances)]
        timed = spectral_mix(own)
        for i in range(instances):
            k = (c * instances + i) * variables + v
            near = state[i, v, 0, 1 - c]
            near = near + jnp.where(row == 0, 0.0, pltpu.roll(own[i], 1, 0))
            near = near + jnp.where(row == axial - 1, 0.0, pltpu.roll(own[i], axial - 1, 0))
            near = near + jnp.where(row == axial_row, axial_ghost[pl.ds(k, 1), :], 0.0)
            near = near + jnp.where(column == 0, 0.0, pltpu.roll(own[i], 1, 1))
            near = near + jnp.where(column == span - 1, 0.0, pltpu.roll(own[i], span - 1, 1))
            edge = take_lanes(columns, jnp.full((axial, LANES), k, jnp.int32))
            edge = jnp.concatenate([edge] * (span // LANES), axis=1)
            near = near + jnp.where(column == span_column, edge, 0.0)
            local = matrix[v, 0, 0, c] * state[i, 0, 0, c]
            for w in range(1, variables):
                local = local + matrix[v, w, 0, c] * state[i, w, 0, c]
            partial[i, v, c] = source[i, v, 0, c] - (local - near + timed[i])


def finish_tile(c, t, ghost, partial, state, matrix, residual, updated, buffers, sems):
    instances, variables, _, axial, _ = partial.shape
    lanes = slice(t * LANES, (t + 1) * LANES)
    copies = [
        pltpu.make_async_copy(buffers.at[n], whole.at[:, :, 0, c, :, lanes], sems.at[n])
        for n, whole in enumerate((residual, updated))
    ]
    right = []
    for i in range(instances):
        right.append([])
        for v in range(variables):
            value = partial[i, v, c, :, lanes] + ghost(i, v, lanes)
            buffers[0, i, v] = value
            right[i].append(value)
    copies[0].start()
    update = solve_tile(right, lambda v, w: matrix[v, w, 0, c, :, lanes], (instances, variables))
    for i in range(instances):
        for v in range(variables):
            buffers[1, i, v] = state[i, v, 0, c, :, lanes] + update[i][v]
    copies[1].start()
    return copies


def near_kernel(partial, state, matrix, ghost, residual, updated, buffers, sems):
    copies = []
    for t in range(partial.shape[-1] // LANES):
        copies += finish_tile(
            places()[0],
            t,
            lambda i, v, lanes: ghost[i, v, :, lanes],
            partial,
            state,
            matrix,
            residual,
            updated,
            buffers.at[t],
            sems.at[t],
        )
    for copy in copies:
        copy.wait()


def far_kernel(t, partial, state, matrix, ghost, paired, _, __, residual, updated, buffers, sems):
    _, far, first, last, _, _ = places()
    copies = finish_tile(
        far,
        t,
        lambda i, v, lanes: jnp.where(first | last, paired[i, v], ghost[i, v, :, lanes]),
        partial,
        state,
        matrix,
        residual,
        updated,
        buffers,
        sems,
    )
    for copy in copies:
        copy.wait()


def call(kernel, name, operands, outs, in_vmem=(), out_vmem=True, scratch=(), aliases=None):
    vmem = pl.BlockSpec(memory_space=pltpu.VMEM)
    anywhere = pl.BlockSpec(memory_space=pl.ANY)
    smem = pl.BlockSpec(memory_space=pltpu.SMEM)
    kinds = {"v": vmem, "a": anywhere, "s": smem}
    return pl.pallas_call(
        kernel,
        name=name,
        in_specs=[kinds[k] for k in in_vmem],
        out_specs=[vmem if out_vmem else anywhere] * len(outs),
        out_shape=outs,
        scratch_shapes=scratch,
        input_output_aliases=aliases or {},
        compiler_params=pltpu.CompilerParams(vmem_limit_bytes=VMEM_LIMIT),
    )(*operands)


def shards(state, source, block_matrix, phase_index, face_pair):
    instances, variables, _, circ, axial, span = state.shape
    tiles = span // LANES
    blocks = lax.axis_size("blocks")
    rings = blocks // AXB

    def array(*shape):
        return jax.ShapeDtypeStruct(shape, jnp.float32)

    def across(block):
        return block ^ 1

    def ring_partner(block, first):
        hop = 1 if block // AXB % 2 == first else -1
        return (block // AXB + hop) % rings * AXB + block % AXB

    def at_end(block):
        return block // AXB in (0, rings - 1)

    every = range(blocks)
    near_route = [(b, ring_partner(b, 0)) for b in every]
    middle_route = [(b, across(b) if at_end(b) else ring_partner(b, 1)) for b in every]
    paired_route = [(b, ring_partner(b, 1) if at_end(b) else across(b)) for b in every]
    axial_route = [(b, across(b)) for b in every]

    layer = array(instances, variables, axial, span)
    far_face, near_face = call(
        split_kernel,
        "split",
        (state,),
        [layer, layer],
        "a",
        scratch=[pltpu.SemaphoreType.DMA((2,))],
    )
    middle_ghost = lax.ppermute(far_face, "blocks", middle_route)
    near_ghost = lax.ppermute(near_face, "blocks", near_route)

    faces = circ * instances * variables
    axial_face, span_face = call(
        faces_kernel, "faces", (state,), [array(faces, span), array(axial, LANES)], "v"
    )
    axial_ghost = lax.ppermute(axial_face, "blocks", axial_route)
    span_ghost = lax.ppermute(span_face, "span", [(0, 1), (1, 0)])

    plus, minus = rotations(phase_index, instances)
    turn = jnp.where(lax.axis_index("blocks") < AXB, plus, minus)
    paired_faces = call(
        paired_kernel,
        "paired",
        (turn, face_pair.reshape(axial, span), state, span_face),
        [array(instances, variables, axial, LANES)] * tiles,
        "svva",
        scratch=[pltpu.VMEM((tiles, axial, LANES), jnp.int32)],
    )
    paired_ghosts = [lax.ppermute(face, "blocks", paired_route) for face in paired_faces]

    (partial,) = call(
        base_kernel,
        "base",
        (state, source, block_matrix, axial_ghost, span_ghost),
        [array(instances, variables, circ, axial, span)],
        "vvvvv",
    )

    out = array(*state.shape)
    tile = (2, instances, variables, axial, LANES)
    residual, updated = call(
        near_kernel,
        "near",
        (partial, state, block_matrix, near_ghost),
        [out, out],
        "vvvv",
        out_vmem=False,
        scratch=[pltpu.VMEM((tiles,) + tile, jnp.float32), pltpu.SemaphoreType.DMA((tiles, 2))],
    )
    for t, ghost in enumerate(paired_ghosts):
        residual, updated = call(
            functools.partial(far_kernel, t),
            "far",
            (partial, state, block_matrix, middle_ghost, ghost, residual, updated),
            [out, out],
            "vvvvvaa",
            out_vmem=False,
            scratch=[pltpu.VMEM(tile, jnp.float32), pltpu.SemaphoreType.DMA((2,))],
            aliases={5: 0, 6: 1},
        )
    return updated, residual


def solution(mesh):
    placed = P(None, None, ("groups", "blocks"), None, None, "span")
    return jax.shard_map(
        shards,
        mesh=mesh,
        in_specs=(placed, placed, placed, P("groups"), P()),
        out_specs=(placed, placed),
        check_vma=False,
    )
```

```python
import functools
import math

import jax
import jax.numpy as jnp
from jax import lax
from jax.experimental import pallas as pl
from jax.experimental.pallas import tpu as pltpu
from jax.sharding import PartitionSpec as P

NPASS = 64
AXB = 2
NSWEEP = 3
LANES = 128
VMEM_LIMIT = 48 * 1024 * 1024


def rotations(phase_index, instances):
    harmonics = (instances - 1) // 2
    spacing = 2.0 * math.pi * jnp.arange(instances, dtype=jnp.float32) / instances
    orders = jnp.arange(1, harmonics + 1, dtype=jnp.float32)
    phases = 2.0 * math.pi * phase_index.astype(jnp.float32) / NPASS
    argument = orders[:, None] * spacing[None]
    plus = (1.0 + 2.0 * jnp.sum(jnp.cos(argument + phases[:, None]), axis=0)) / instances
    minus = (1.0 + 2.0 * jnp.sum(jnp.cos(argument - phases[:, None]), axis=0)) / instances
    return plus, minus


def spectral_weights(instances):
    harmonics = (instances - 1) // 2
    return [
        -(2.0 / instances)
        * sum(k * math.sin(2.0 * math.pi * k * d / instances) for k in range(1, harmonics + 1))
        for d in range(1, harmonics + 1)
    ]


def spectral_mix(values):
    count = len(values)
    mixed = []
    for n in range(count):
        total = None
        for d, weight in enumerate(spectral_weights(count), 1):
            term = weight * (values[(n - d) % count] - values[(n + d) % count])
            total = term if total is None else total + term
        mixed.append(total)
    return mixed


def take_lanes(tile, index):
    return jnp.take_along_axis(tile, index, axis=1, mode="promise_in_bounds")


def inverse_pairing(pairing):
    axial, span = pairing.shape
    tiles = span // LANES
    rows = axial * tiles
    row = lax.broadcasted_iota(jnp.int32, (rows, span), 0)
    wanted_row = (row % axial) * tiles + row // axial
    place = lax.broadcasted_iota(jnp.int32, (rows, span), 1)
    lane = lax.broadcasted_iota(jnp.int32, (LANES, span), 0)
    total = jnp.zeros((2 * rows, LANES), jnp.float32)
    for a in range(axial):
        target = pairing[a : a + 1]
        hit = wanted_row == target // LANES
        origin = place + a * span
        high = jnp.where(hit, origin // LANES, 0)
        low = jnp.where(hit, origin % LANES, 0)
        left = jnp.concatenate([high, low], axis=0).astype(jnp.float32).astype(jnp.bfloat16)
        right = (lane == target % LANES).astype(jnp.float32).astype(jnp.bfloat16)
        total = total + lax.dot_general(
            left, right, (((1,), (1,)), ((), ())), preferred_element_type=jnp.float32
        )
    cells = (total[:rows] * LANES + total[rows:]).astype(jnp.int32)
    return [cells[t * axial : (t + 1) * axial] for t in range(tiles)]


def places():
    rings = lax.axis_size("blocks") // AXB
    position = lax.axis_index("blocks")
    ring = position // AXB
    near = 1 - ring % 2
    return near, 1 - near, ring == 0, ring == rings - 1, position % AXB, lax.axis_index("span")


def layer_kernel(kind, state, *refs):
    face = refs[-1]
    c = places()[kind]
    for i in range(state.shape[0]):
        for v in range(state.shape[1]):
            face[i, v] = state[i, v, 0, c]


def paired_kernel(turn, pairing, state, _, *outs_and_scratch):
    *outs, index = outs_and_scratch
    instances, variables, _, _, axial, span = state.shape
    tiles = span // LANES
    _, far, first, last, _, _ = places()

    @pl.when(first)
    def _():
        for t, cells in enumerate(inverse_pairing(pairing[...])):
            index[t] = cells

    @pl.when(last)
    def _():
        for t in range(tiles):
            index[t] = pairing[:, t * LANES : (t + 1) * LANES]

    @pl.when(first | last)
    def _():
        for t, out in enumerate(outs):
            lane = index[t] % LANES
            row = index[t] // LANES

            @pl.loop(0, variables)
            def _(v):
                picked = [jnp.zeros((axial, LANES), jnp.float32)] * instances
                for a in range(axial):
                    for s in range(tiles):
                        hit = row == a * tiles + s
                        for i in range(instances):
                            line = state[i, v, 0, far, a : a + 1, s * LANES : (s + 1) * LANES]
                            line = jnp.broadcast_to(line, (axial, LANES))
                            picked[i] = jnp.where(hit, take_lanes(line, lane), picked[i])
                for n in range(instances):
                    total = turn[n : n + 1] * picked[0]
                    for m in range(1, instances):
                        k = (n - m) % instances
                        total = total + turn[k : k + 1] * picked[m]
                    out[n, v] = total


def faces_kernel(state, _, axial_face, span_face):
    instances, variables, _, circ, axial, span = state.shape
    _, _, _, _, axial_place, span_place = places()
    edge = jnp.where(axial_place == 0, axial - 1, 0)
    last = (span_place == 0).astype(jnp.int32)
    lane = lax.broadcasted_iota(jnp.int32, (axial, LANES), 1)
    edge_lane = jnp.full((axial, LANES), last * (LANES - 1), jnp.int32)
    start = pl.multiple_of(last * (span - LANES), LANES)
    columns = jnp.zeros((axial, LANES), jnp.float32)
    for c in range(circ):
        for i in range(instances):
            for v in range(variables):
                k = (c * instances + i) * variables + v
                axial_face[k : k + 1] = state[i, v, 0, c, pl.ds(edge, 1), :]
                tile = take_lanes(state[i, v, 0, c, :, pl.ds(start, LANES)], edge_lane)
                columns = jnp.where(lane == k, tile, columns)
    span_face[...] = columns


def solve_tile(residual, matrix, count):
    instances, variables = count
    scale = [1.0 / matrix(v, v) for v in range(variables)]
    first = [[residual[i][v] * scale[v] for v in range(variables)] for i in range(instances)]
    update = first
    for _ in range(NSWEEP):
        later = [[None] * variables for _ in range(instances)]
        for v in range(variables):
            total = spectral_mix([update[i][v] for i in range(instances)])
            for w in range(variables):
                if w != v:
                    entry = matrix(v, w)
                    for i in range(instances):
                        total[i] = total[i] + entry * update[i][w]
            for i in range(instances):
                later[i][v] = first[i][v] - scale[v] * total[i]
        update = later
    return update


def base_kernel(state, source, matrix, partial):
    instances, variables, _, circ, axial, span = state.shape
    row = lax.broadcasted_iota(jnp.int32, (axial, span), 0)
    column = lax.broadcasted_iota(jnp.int32, (axial, span), 1)

    @pl.loop(0, circ * variables)
    def _(step):
        c = step // variables
        v = step % variables
        own = [state[i, v, 0, c] for i in range(instances)]
        timed = spectral_mix(own)
        for i in range(instances):
            near = state[i, v, 0, 1 - c]
            near = near + jnp.where(row == 0, 0.0, pltpu.roll(own[i], 1, 0))
            near = near + jnp.where(row == axial - 1, 0.0, pltpu.roll(own[i], axial - 1, 0))
            near = near + jnp.where(column == 0, 0.0, pltpu.roll(own[i], 1, 1))
            near = near + jnp.where(column == span - 1, 0.0, pltpu.roll(own[i], span - 1, 1))
            local = matrix[v, 0, 0, c] * state[i, 0, 0, c]
            for w in range(1, variables):
                local = local + matrix[v, w, 0, c] * state[i, w, 0, c]
            partial[i, v, c] = source[i, v, 0, c] - (local - near + timed[i])


def edge_adder(shape, axial_ghost, span_ghost):
    instances, variables, axial, span = shape
    _, _, _, _, axial_place, span_place = places()
    row = lax.broadcasted_iota(jnp.int32, (axial, span), 0)
    column = lax.broadcasted_iota(jnp.int32, (axial, span), 1)
    at_row = row == jnp.where(axial_place == 0, axial - 1, 0)
    at_column = column == jnp.where(span_place == 0, span - 1, 0)
    columns = span_ghost[...]

    def add(value, c, i, v):
        k = (c * instances + i) * variables + v
        edge = take_lanes(columns, jnp.full((axial, LANES), k, jnp.int32))
        edge = jnp.concatenate([edge] * (span // LANES), axis=1)
        value = value + jnp.where(at_row, axial_ghost[pl.ds(k, 1), :], 0.0)
        return value + jnp.where(at_column, edge, 0.0)

    return add


def finish_tile(c, t, right, state, matrix, residual, updated, buffers, sems):
    instances, variables = state.shape[:2]
    lanes = slice(t * LANES, (t + 1) * LANES)
    copies = [
        pltpu.make_async_copy(buffers.at[n], whole.at[:, :, 0, c, :, lanes], sems.at[n])
        for n, whole in enumerate((residual, updated))
    ]
    values = []
    for i in range(instances):
        values.append([])
        for v in range(variables):
            value = right(i, v, lanes)
            buffers[0, i, v] = value
            values[i].append(value)
    copies[0].start()
    update = solve_tile(values, lambda v, w: matrix[v, w, 0, c, :, lanes], (instances, variables))
    for i in range(instances):
        for v in range(variables):
            buffers[1, i, v] = state[i, v, 0, c, :, lanes] + update[i][v]
    copies[1].start()
    return copies


def near_kernel(
    partial,
    state,
    matrix,
    near_ghost,
    middle_ghost,
    axial_ghost,
    span_ghost,
    residual,
    updated,
    waiting,
    buffers,
    sems,
    total,
):
    near, far, first, last, _, _ = places()
    shape = near_ghost.shape
    add = edge_adder(shape, axial_ghost, span_ghost)

    @pl.loop(0, shape[1])
    def _(v):
        for i in range(shape[0]):
            total[i, v] = add(partial[i, v, near], near, i, v) + near_ghost[i, v]

    copies = []
    for t in range(shape[-1] // LANES):
        copies += finish_tile(
            near,
            t,
            lambda i, v, lanes: total[i, v, :, lanes],
            state,
            matrix,
            residual,
            updated,
            buffers.at[t],
            sems.at[t],
        )

    @pl.loop(0, shape[1])
    def _(v):
        for i in range(shape[0]):
            ghost = jnp.where(first | last, 0.0, middle_ghost[i, v])
            waiting[i, v] = add(partial[i, v, far], far, i, v) + ghost

    for copy in copies:
        copy.wait()


def far_kernel(t, waiting, state, matrix, paired, _, __, residual, updated, buffers, sems):
    _, far, first, last, _, _ = places()
    copies = finish_tile(
        far,
        t,
        lambda i, v, lanes: waiting[i, v, :, lanes] + jnp.where(first | last, paired[i, v], 0.0),
        state,
        matrix,
        residual,
        updated,
        buffers,
        sems,
    )
    for copy in copies:
        copy.wait()


def call(kernel, name, operands, outs, ins, out_kinds=None, scratch=(), aliases=None):
    vmem = pl.BlockSpec(memory_space=pltpu.VMEM)
    anywhere = pl.BlockSpec(memory_space=pl.ANY)
    smem = pl.BlockSpec(memory_space=pltpu.SMEM)
    kinds = {"v": vmem, "a": anywhere, "s": smem}
    return pl.pallas_call(
        kernel,
        name=name,
        in_specs=[kinds[k] for k in ins],
        out_specs=[kinds[k] for k in out_kinds or "v" * len(outs)],
        out_shape=outs,
        scratch_shapes=scratch,
        input_output_aliases=aliases or {},
        compiler_params=pltpu.CompilerParams(vmem_limit_bytes=VMEM_LIMIT),
    )(*operands)


def shards(state, source, block_matrix, phase_index, face_pair):
    instances, variables, _, circ, axial, span = state.shape
    tiles = span // LANES
    blocks = lax.axis_size("blocks")
    cores = lax.axis_size("span")
    rings = blocks // AXB

    def array(*shape):
        return jax.ShapeDtypeStruct(shape, jnp.float32)

    def ring_partner(block, first):
        hop = 1 if block // AXB % 2 == first else -1
        return (block // AXB + hop) % rings * AXB + block % AXB

    def far_route(ends):
        route = []
        for block in range(blocks):
            for core in range(cores):
                if (block // AXB in (0, rings - 1)) == ends:
                    target = ring_partner(block, 1) * cores + core
                else:
                    target = block * cores + (core ^ 1)
                route.append((block * cores + core, target))
        return route

    both = ("blocks", "span")
    near_route = [(b, ring_partner(b, 0)) for b in range(blocks)]
    axial_route = [(b, b ^ 1) for b in range(blocks)]

    layer = array(instances, variables, axial, span)
    (far_face,) = call(
        functools.partial(layer_kernel, 1), "far_layer", (state,), [layer], "v"
    )
    (near_face,) = call(
        functools.partial(layer_kernel, 0), "near_layer", (state, far_face), [layer], "va"
    )
    middle_ghost = lax.ppermute(far_face, both, far_route(False))
    near_ghost = lax.ppermute(near_face, "blocks", near_route)

    faces = circ * instances * variables
    axial_face, span_face = call(
        faces_kernel,
        "faces",
        (state, near_face),
        [array(faces, span), array(axial, LANES)],
        "va",
    )
    axial_ghost = lax.ppermute(axial_face, "blocks", axial_route)
    span_ghost = lax.ppermute(span_face, "span", [(0, 1), (1, 0)])

    plus, minus = rotations(phase_index, instances)
    turn = jnp.where(lax.axis_index("blocks") < AXB, plus, minus)
    turn = jnp.broadcast_to(turn[:, None], (instances, LANES))
    chunks = [array(instances, variables, axial, LANES)] * tiles
    paired_faces = call(
        paired_kernel,
        "paired",
        (turn, face_pair.reshape(axial, span), state, span_face),
        chunks,
        "vvva",
        scratch=[pltpu.VMEM((tiles, axial, LANES), jnp.int32)],
    )
    paired_ghosts = [lax.ppermute(face, both, far_route(True)) for face in paired_faces]

    (partial,) = call(
        base_kernel,
        "base",
        (state, source, block_matrix),
        [array(instances, variables, circ, axial, span)],
        "vvv",
    )
    out = array(*state.shape)
    tile = (2, instances, variables, axial, LANES)
    residual, updated, waiting = call(
        near_kernel,
        "near",
        (partial, state, block_matrix, near_ghost, middle_ghost, axial_ghost, span_ghost),
        [out, out, layer],
        "vvvvvvv",
        "aav",
        [
            pltpu.VMEM((tiles,) + tile, jnp.float32),
            pltpu.SemaphoreType.DMA((tiles, 2)),
            pltpu.VMEM(layer.shape, jnp.float32),
        ],
    )
    for t, ghost in enumerate(paired_ghosts):
        residual, updated = call(
            functools.partial(far_kernel, t),
            "far",
            (waiting, state, block_matrix, ghost, residual, updated),
            [out, out],
            "vvvvaa",
            "aa",
            [pltpu.VMEM(tile, jnp.float32), pltpu.SemaphoreType.DMA((2,))],
            {4: 0, 5: 1},
        )
    return updated, residual


def solution(mesh):
    placed = P(None, None, ("groups", "blocks"), None, None, "span")
    return jax.shard_map(
        shards,
        mesh=mesh,
        in_specs=(placed, placed, placed, P("groups"), P()),
        out_specs=(placed, placed),
        check_vma=False,
    )
```

```python
import functools
import math

import jax
import jax.numpy as jnp
from jax import lax
from jax.experimental import pallas as pl
from jax.experimental.pallas import tpu as pltpu
from jax.sharding import PartitionSpec as P

NPASS = 64
AXB = 2
NSWEEP = 3
LANES = 128
VMEM_LIMIT = 48 * 1024 * 1024


def rotations(phase_index, instances):
    harmonics = (instances - 1) // 2
    spacing = 2.0 * math.pi * jnp.arange(instances, dtype=jnp.float32) / instances
    orders = jnp.arange(1, harmonics + 1, dtype=jnp.float32)
    phases = 2.0 * math.pi * phase_index.astype(jnp.float32) / NPASS
    argument = orders[:, None] * spacing[None]
    plus = (1.0 + 2.0 * jnp.sum(jnp.cos(argument + phases[:, None]), axis=0)) / instances
    minus = (1.0 + 2.0 * jnp.sum(jnp.cos(argument - phases[:, None]), axis=0)) / instances
    return plus, minus


def spectral_weights(instances):
    harmonics = (instances - 1) // 2
    return [
        -(2.0 / instances)
        * sum(k * math.sin(2.0 * math.pi * k * d / instances) for k in range(1, harmonics + 1))
        for d in range(1, harmonics + 1)
    ]


def spectral_mix(values):
    count = len(values)
    mixed = []
    for n in range(count):
        total = None
        for d, weight in enumerate(spectral_weights(count), 1):
            term = weight * (values[(n - d) % count] - values[(n + d) % count])
            total = term if total is None else total + term
        mixed.append(total)
    return mixed


def take_lanes(tile, index):
    return jnp.take_along_axis(tile, index, axis=1, mode="promise_in_bounds")


def inverse_pairing(pairing):
    axial, span = pairing.shape
    tiles = span // LANES
    rows = axial * tiles
    row = lax.broadcasted_iota(jnp.int32, (rows, span), 0)
    wanted_row = (row % axial) * tiles + row // axial
    place = lax.broadcasted_iota(jnp.int32, (rows, span), 1)
    lane = lax.broadcasted_iota(jnp.int32, (LANES, span), 0)
    total = jnp.zeros((2 * rows, LANES), jnp.float32)
    for a in range(axial):
        target = pairing[a : a + 1]
        hit = wanted_row == target // LANES
        origin = place + a * span
        high = jnp.where(hit, origin // LANES, 0)
        low = jnp.where(hit, origin % LANES, 0)
        left = jnp.concatenate([high, low], axis=0).astype(jnp.float32).astype(jnp.bfloat16)
        right = (lane == target % LANES).astype(jnp.float32).astype(jnp.bfloat16)
        total = total + lax.dot_general(
            left, right, (((1,), (1,)), ((), ())), preferred_element_type=jnp.float32
        )
    cells = (total[:rows] * LANES + total[rows:]).astype(jnp.int32)
    return [cells[t * axial : (t + 1) * axial] for t in range(tiles)]


def places():
    rings = lax.axis_size("blocks") // AXB
    position = lax.axis_index("blocks")
    ring = position // AXB
    near = 1 - ring % 2
    return near, 1 - near, ring == 0, ring == rings - 1, position % AXB, lax.axis_index("span")


def layer_kernel(kind, state, *refs):
    face = refs[-1]
    c = places()[kind]
    for i in range(state.shape[0]):
        for v in range(state.shape[1]):
            face[i, v] = state[i, v, 0, c]


def paired_kernel(turn, pairing, state, _, *outs_and_scratch):
    *outs, index = outs_and_scratch
    instances, variables, _, _, axial, span = state.shape
    tiles = span // LANES
    _, far, first, last, _, _ = places()

    @pl.when(first)
    def _():
        for t, cells in enumerate(inverse_pairing(pairing[...])):
            index[t] = cells

    @pl.when(last)
    def _():
        for t in range(tiles):
            index[t] = pairing[:, t * LANES : (t + 1) * LANES]

    @pl.when(first | last)
    def _():
        for t, out in enumerate(outs):
            lane = index[t] % LANES
            row = index[t] // LANES

            @pl.loop(0, variables)
            def _(v):
                picked = [jnp.zeros((axial, LANES), jnp.float32)] * instances
                for a in range(axial):
                    for s in range(tiles):
                        hit = row == a * tiles + s
                        for i in range(instances):
                            line = state[i, v, 0, far, a : a + 1, s * LANES : (s + 1) * LANES]
                            line = jnp.broadcast_to(line, (axial, LANES))
                            picked[i] = jnp.where(hit, take_lanes(line, lane), picked[i])
                for n in range(instances):
                    total = turn[n : n + 1] * picked[0]
                    for m in range(1, instances):
                        k = (n - m) % instances
                        total = total + turn[k : k + 1] * picked[m]
                    out[n, v] = total


def faces_kernel(state, _, axial_face, span_face):
    instances, variables, _, circ, axial, span = state.shape
    _, _, _, _, axial_place, span_place = places()
    edge = jnp.where(axial_place == 0, axial - 1, 0)
    last = (span_place == 0).astype(jnp.int32)
    lane = lax.broadcasted_iota(jnp.int32, (axial, LANES), 1)
    edge_lane = jnp.full((axial, LANES), last * (LANES - 1), jnp.int32)
    start = pl.multiple_of(last * (span - LANES), LANES)
    columns = jnp.zeros((axial, LANES), jnp.float32)
    for c in range(circ):
        for i in range(instances):
            for v in range(variables):
                k = (c * instances + i) * variables + v
                axial_face[k : k + 1] = state[i, v, 0, c, pl.ds(edge, 1), :]
                tile = take_lanes(state[i, v, 0, c, :, pl.ds(start, LANES)], edge_lane)
                columns = jnp.where(lane == k, tile, columns)
    span_face[...] = columns


def harmonic_tables(instances):
    harmonics = range(1, (instances - 1) // 2 + 1)
    turn = 2.0 * math.pi / instances
    cosines = [[math.cos(turn * k * n) for n in harmonics] for k in harmonics]
    sines = [[math.sin(turn * k * n) for n in harmonics] for k in harmonics]
    return cosines, sines


def weighted(weights, values):
    total = weights[0] * values[0]
    for weight, value in zip(weights[1:], values[1:]):
        total = total + weight * value
    return total


def to_harmonics(values):
    count = len(values)
    half = range(1, (count - 1) // 2 + 1)
    cosines, sines = harmonic_tables(count)
    even = [values[n] + values[count - n] for n in half]
    odd = [values[n] - values[count - n] for n in half]
    modes = [sum(even[1:], values[0] + even[0])]
    for k in range(len(half)):
        modes.append(values[0] + weighted(cosines[k], even))
        modes.append(weighted(sines[k], odd))
    return modes


def from_harmonics(modes):
    count = len(modes)
    harmonics = range((count - 1) // 2)
    cosines, sines = harmonic_tables(count)
    mean = modes[0] * (1.0 / count)
    cosine = [modes[2 * k + 1] * (2.0 / count) for k in harmonics]
    sine = [modes[2 * k + 2] * (2.0 / count) for k in harmonics]
    values = [None] * count
    values[0] = sum(cosine[1:], mean + cosine[0])
    for n in harmonics:
        even = mean + weighted([cosines[k][n] for k in harmonics], cosine)
        odd = weighted([sines[k][n] for k in harmonics], sine)
        values[n + 1] = even + odd
        values[count - n - 1] = even - odd
    return values


def solve_tile(residual, matrix, count):
    instances, variables = count
    scale = [1.0 / matrix(v, v) for v in range(variables)]
    first = [
        [mode * scale[v] for mode in to_harmonics([residual[i][v] for i in range(instances)])]
        for v in range(variables)
    ]
    update = first
    for _ in range(NSWEEP):
        later = []
        for v in range(variables):
            total = [None] * instances
            for k in range(1, (instances - 1) // 2 + 1):
                total[2 * k - 1] = float(k) * update[v][2 * k]
                total[2 * k] = -float(k) * update[v][2 * k - 1]
            for w in range(variables):
                if w != v:
                    entry = matrix(v, w)
                    for m in range(instances):
                        term = entry * update[w][m]
                        total[m] = term if total[m] is None else total[m] + term
            later.append([first[v][m] - scale[v] * total[m] for m in range(instances)])
        update = later
    solved = [from_harmonics(modes) for modes in update]
    return [[solved[v][i] for v in range(variables)] for i in range(instances)]


def base_kernel(state, source, matrix, axial_ghost, span_ghost, partial):
    instances, variables, _, circ, axial, span = state.shape
    _, _, _, _, axial_place, span_place = places()
    row = lax.broadcasted_iota(jnp.int32, (axial, span), 0)
    column = lax.broadcasted_iota(jnp.int32, (axial, span), 1)
    axial_row = jnp.where(axial_place == 0, axial - 1, 0)
    span_column = jnp.where(span_place == 0, span - 1, 0)
    columns = span_ghost[...]

    @pl.loop(0, circ * variables)
    def _(step):
        c = step // variables
        v = step % variables
        own = [state[i, v, 0, c] for i in range(instances)]
        timed = spectral_mix(own)
        for i in range(instances):
            k = (c * instances + i) * variables + v
            near = state[i, v, 0, 1 - c]
            near = near + jnp.where(row == 0, 0.0, pltpu.roll(own[i], 1, 0))
            near = near + jnp.where(row == axial - 1, 0.0, pltpu.roll(own[i], axial - 1, 0))
            near = near + jnp.where(row == axial_row, axial_ghost[pl.ds(k, 1), :], 0.0)
            near = near + jnp.where(column == 0, 0.0, pltpu.roll(own[i], 1, 1))
            near = near + jnp.where(column == span - 1, 0.0, pltpu.roll(own[i], span - 1, 1))
            edge = take_lanes(columns, jnp.full((axial, LANES), k, jnp.int32))
            edge = jnp.concatenate([edge] * (span // LANES), axis=1)
            near = near + jnp.where(column == span_column, edge, 0.0)
            local = matrix[v, 0, 0, c] * state[i, 0, 0, c]
            for w in range(1, variables):
                local = local + matrix[v, w, 0, c] * state[i, w, 0, c]
            partial[i, v, c] = source[i, v, 0, c] - (local - near + timed[i])


def finish_tile(c, t, right, state, matrix, residual, updated, buffers, sems):
    instances, variables = state.shape[:2]
    lanes = slice(t * LANES, (t + 1) * LANES)
    copies = [
        pltpu.make_async_copy(buffers.at[n], whole.at[:, :, 0, c, :, lanes], sems.at[n])
        for n, whole in enumerate((residual, updated))
    ]
    values = []
    for i in range(instances):
        values.append([])
        for v in range(variables):
            value = right(i, v, lanes)
            buffers[0, i, v] = value
            values[i].append(value)
    copies[0].start()
    update = solve_tile(values, lambda v, w: matrix[v, w, 0, c, :, lanes], (instances, variables))
    for i in range(instances):
        for v in range(variables):
            buffers[1, i, v] = state[i, v, 0, c, :, lanes] + update[i][v]
    copies[1].start()
    return copies


def near_kernel(partial, state, matrix, ghost, residual, updated, buffers, sems):
    near = places()[0]
    copies = []
    for t in range(partial.shape[-1] // LANES):
        copies += finish_tile(
            near,
            t,
            lambda i, v, lanes: partial[i, v, near, :, lanes] + ghost[i, v, :, lanes],
            state,
            matrix,
            residual,
            updated,
            buffers.at[t],
            sems.at[t],
        )
    for copy in copies:
        copy.wait()


def far_kernel(t, partial, state, matrix, middle, paired, _, __, residual, updated, buffers, sems):
    _, far, first, last, _, _ = places()

    def right(i, v, lanes):
        ghost = jnp.where(first | last, paired[i, v], middle[i, v, :, lanes])
        return partial[i, v, far, :, lanes] + ghost

    copies = finish_tile(far, t, right, state, matrix, residual, updated, buffers, sems)
    for copy in copies:
        copy.wait()


def call(kernel, name, operands, outs, ins, out_kinds=None, scratch=(), aliases=None):
    vmem = pl.BlockSpec(memory_space=pltpu.VMEM)
    anywhere = pl.BlockSpec(memory_space=pl.ANY)
    smem = pl.BlockSpec(memory_space=pltpu.SMEM)
    kinds = {"v": vmem, "a": anywhere, "s": smem}
    return pl.pallas_call(
        kernel,
        name=name,
        in_specs=[kinds[k] for k in ins],
        out_specs=[kinds[k] for k in out_kinds or "v" * len(outs)],
        out_shape=outs,
        scratch_shapes=scratch,
        input_output_aliases=aliases or {},
        compiler_params=pltpu.CompilerParams(vmem_limit_bytes=VMEM_LIMIT),
    )(*operands)


def shards(state, source, block_matrix, phase_index, face_pair):
    instances, variables, _, circ, axial, span = state.shape
    tiles = span // LANES
    blocks = lax.axis_size("blocks")
    cores = lax.axis_size("span")
    rings = blocks // AXB

    def array(*shape):
        return jax.ShapeDtypeStruct(shape, jnp.float32)

    def ring_partner(block, first):
        hop = 1 if block // AXB % 2 == first else -1
        return (block // AXB + hop) % rings * AXB + block % AXB

    def far_route(ends):
        route = []
        for block in range(blocks):
            for core in range(cores):
                if (block // AXB in (0, rings - 1)) == ends:
                    target = ring_partner(block, 1) * cores + core
                else:
                    target = block * cores + (core ^ 1)
                route.append((block * cores + core, target))
        return route

    both = ("blocks", "span")
    near_route = [(b, ring_partner(b, 0)) for b in range(blocks)]
    axial_route = [(b, b ^ 1) for b in range(blocks)]

    layer = array(instances, variables, axial, span)
    (near_face,) = call(
        functools.partial(layer_kernel, 0), "near_layer", (state,), [layer], "v"
    )
    near_ghost = lax.ppermute(near_face, "blocks", near_route)
    (far_face,) = call(
        functools.partial(layer_kernel, 1), "far_layer", (state, near_face), [layer], "va"
    )
    middle_ghost = lax.ppermute(far_face, both, far_route(False))

    faces = circ * instances * variables
    axial_face, span_face = call(
        faces_kernel,
        "faces",
        (state, far_face),
        [array(faces, span), array(axial, LANES)],
        "va",
    )
    axial_ghost = lax.ppermute(axial_face, "blocks", axial_route)
    span_ghost = lax.ppermute(span_face, "span", [(0, 1), (1, 0)])

    plus, minus = rotations(phase_index, instances)
    turn = jnp.where(lax.axis_index("blocks") < AXB, plus, minus)
    turn = jnp.broadcast_to(turn[:, None], (instances, LANES))
    chunks = [array(instances, variables, axial, LANES)] * tiles
    paired_faces = call(
        paired_kernel,
        "paired",
        (turn, face_pair.reshape(axial, span), state, span_face),
        chunks,
        "vvva",
        scratch=[pltpu.VMEM((tiles, axial, LANES), jnp.int32)],
    )
    paired_ghosts = [lax.ppermute(face, both, far_route(True)) for face in paired_faces]

    (partial,) = call(
        base_kernel,
        "base",
        (state, source, block_matrix, axial_ghost, span_ghost),
        [array(instances, variables, circ, axial, span)],
        "vvvvv",
    )
    out = array(*state.shape)
    tile = (2, instances, variables, axial, LANES)
    residual, updated = call(
        near_kernel,
        "near",
        (partial, state, block_matrix, near_ghost),
        [out, out],
        "vvvv",
        "aa",
        [pltpu.VMEM((tiles,) + tile, jnp.float32), pltpu.SemaphoreType.DMA((tiles, 2))],
    )
    for t, ghost in enumerate(paired_ghosts):
        residual, updated = call(
            functools.partial(far_kernel, t),
            "far",
            (partial, state, block_matrix, middle_ghost, ghost, residual, updated),
            [out, out],
            "vvvvvaa",
            "aa",
            [pltpu.VMEM(tile, jnp.float32), pltpu.SemaphoreType.DMA((2,))],
            {5: 0, 6: 1},
        )
    return updated, residual


def solution(mesh):
    placed = P(None, None, ("groups", "blocks"), None, None, "span")
    return jax.shard_map(
        shards,
        mesh=mesh,
        in_specs=(placed, placed, placed, P("groups"), P()),
        out_specs=(placed, placed),
        check_vma=False,
    )
```

```python
import functools
import math

import jax
import jax.numpy as jnp
from jax import lax
from jax.experimental import pallas as pl
from jax.experimental.pallas import tpu as pltpu
from jax.sharding import PartitionSpec as P

NPASS = 64
AXB = 2
NSWEEP = 3
LANES = 128
VMEM_LIMIT = 48 * 1024 * 1024


def rotations(phase_index, instances):
    harmonics = (instances - 1) // 2
    spacing = 2.0 * math.pi * jnp.arange(instances, dtype=jnp.float32) / instances
    orders = jnp.arange(1, harmonics + 1, dtype=jnp.float32)
    phases = 2.0 * math.pi * phase_index.astype(jnp.float32) / NPASS
    argument = orders[:, None] * spacing[None]
    plus = (1.0 + 2.0 * jnp.sum(jnp.cos(argument + phases[:, None]), axis=0)) / instances
    minus = (1.0 + 2.0 * jnp.sum(jnp.cos(argument - phases[:, None]), axis=0)) / instances
    return plus, minus


def spectral_weights(instances):
    harmonics = (instances - 1) // 2
    return [
        -(2.0 / instances)
        * sum(k * math.sin(2.0 * math.pi * k * d / instances) for k in range(1, harmonics + 1))
        for d in range(1, harmonics + 1)
    ]


def spectral_mix(values):
    count = len(values)
    mixed = []
    for n in range(count):
        total = None
        for d, weight in enumerate(spectral_weights(count), 1):
            term = weight * (values[(n - d) % count] - values[(n + d) % count])
            total = term if total is None else total + term
        mixed.append(total)
    return mixed


def take_lanes(tile, index):
    return jnp.take_along_axis(tile, index, axis=1, mode="promise_in_bounds")


def inverse_pairing(pairing):
    axial, span = pairing.shape
    tiles = span // LANES
    rows = axial * tiles
    row = lax.broadcasted_iota(jnp.int32, (rows, span), 0)
    wanted_row = (row % axial) * tiles + row // axial
    place = lax.broadcasted_iota(jnp.int32, (rows, span), 1)
    lane = lax.broadcasted_iota(jnp.int32, (LANES, span), 0)
    total = jnp.zeros((2 * rows, LANES), jnp.float32)
    for a in range(axial):
        target = pairing[a : a + 1]
        hit = wanted_row == target // LANES
        origin = place + a * span
        high = jnp.where(hit, origin // LANES, 0)
        low = jnp.where(hit, origin % LANES, 0)
        left = jnp.concatenate([high, low], axis=0).astype(jnp.float32).astype(jnp.bfloat16)
        right = (lane == target % LANES).astype(jnp.float32).astype(jnp.bfloat16)
        total = total + lax.dot_general(
            left, right, (((1,), (1,)), ((), ())), preferred_element_type=jnp.float32
        )
    cells = (total[:rows] * LANES + total[rows:]).astype(jnp.int32)
    return [cells[t * axial : (t + 1) * axial] for t in range(tiles)]


def places():
    rings = lax.axis_size("blocks") // AXB
    position = lax.axis_index("blocks")
    ring = position // AXB
    near = 1 - ring % 2
    return near, 1 - near, ring == 0, ring == rings - 1, position % AXB, lax.axis_index("span")


def layer_kernel(kind, state, *refs):
    face = refs[-1]
    c = places()[kind]
    for i in range(state.shape[0]):
        for v in range(state.shape[1]):
            face[i, v] = state[i, v, 0, c]


def paired_kernel(turn, pairing, state, _, *outs_and_scratch):
    *outs, index = outs_and_scratch
    instances, variables, _, _, axial, span = state.shape
    tiles = span // LANES
    _, far, first, last, _, _ = places()

    @pl.when(first)
    def _():
        for t, cells in enumerate(inverse_pairing(pairing[...])):
            index[t] = cells

    @pl.when(last)
    def _():
        for t in range(tiles):
            index[t] = pairing[:, t * LANES : (t + 1) * LANES]

    @pl.when(first | last)
    def _():
        for t, out in enumerate(outs):
            lane = index[t] % LANES
            row = index[t] // LANES

            @pl.loop(0, variables)
            def _(v):
                picked = [jnp.zeros((axial, LANES), jnp.float32)] * instances
                for a in range(axial):
                    for s in range(tiles):
                        hit = row == a * tiles + s
                        for i in range(instances):
                            line = state[i, v, 0, far, a : a + 1, s * LANES : (s + 1) * LANES]
                            line = jnp.broadcast_to(line, (axial, LANES))
                            picked[i] = jnp.where(hit, take_lanes(line, lane), picked[i])
                for n in range(instances):
                    total = turn[n : n + 1] * picked[0]
                    for m in range(1, instances):
                        k = (n - m) % instances
                        total = total + turn[k : k + 1] * picked[m]
                    out[n, v] = total


def faces_kernel(state, _, axial_face, span_face):
    instances, variables, _, circ, axial, span = state.shape
    _, _, _, _, axial_place, span_place = places()
    edge = jnp.where(axial_place == 0, axial - 1, 0)
    last = (span_place == 0).astype(jnp.int32)
    lane = lax.broadcasted_iota(jnp.int32, (axial, LANES), 1)
    edge_lane = jnp.full((axial, LANES), last * (LANES - 1), jnp.int32)
    start = pl.multiple_of(last * (span - LANES), LANES)
    columns = jnp.zeros((axial, LANES), jnp.float32)
    for c in range(circ):
        for i in range(instances):
            for v in range(variables):
                k = (c * instances + i) * variables + v
                axial_face[k : k + 1] = state[i, v, 0, c, pl.ds(edge, 1), :]
                tile = take_lanes(state[i, v, 0, c, :, pl.ds(start, LANES)], edge_lane)
                columns = jnp.where(lane == k, tile, columns)
    span_face[...] = columns


def harmonic_tables(instances):
    harmonics = range(1, (instances - 1) // 2 + 1)
    turn = 2.0 * math.pi / instances
    cosines = [[math.cos(turn * k * n) for n in harmonics] for k in harmonics]
    sines = [[math.sin(turn * k * n) for n in harmonics] for k in harmonics]
    return cosines, sines


def weighted(weights, values):
    total = weights[0] * values[0]
    for weight, value in zip(weights[1:], values[1:]):
        total = total + weight * value
    return total


def to_harmonics(values):
    count = len(values)
    half = range(1, (count - 1) // 2 + 1)
    cosines, sines = harmonic_tables(count)
    even = [values[n] + values[count - n] for n in half]
    odd = [values[n] - values[count - n] for n in half]
    modes = [sum(even[1:], values[0] + even[0])]
    for k in range(len(half)):
        modes.append(values[0] + weighted(cosines[k], even))
        modes.append(weighted(sines[k], odd))
    return modes


def from_harmonics(modes):
    count = len(modes)
    harmonics = range((count - 1) // 2)
    cosines, sines = harmonic_tables(count)
    mean = modes[0] * (1.0 / count)
    cosine = [modes[2 * k + 1] * (2.0 / count) for k in harmonics]
    sine = [modes[2 * k + 2] * (2.0 / count) for k in harmonics]
    values = [None] * count
    values[0] = sum(cosine[1:], mean + cosine[0])
    for n in harmonics:
        even = mean + weighted([cosines[k][n] for k in harmonics], cosine)
        odd = weighted([sines[k][n] for k in harmonics], sine)
        values[n + 1] = even + odd
        values[count - n - 1] = even - odd
    return values


def solve_tile(residual, matrix, count):
    instances, variables = count
    scale = [1.0 / matrix(v, v) for v in range(variables)]
    first = [
        [mode * scale[v] for mode in to_harmonics([residual[i][v] for i in range(instances)])]
        for v in range(variables)
    ]
    update = first
    for _ in range(NSWEEP):
        later = []
        for v in range(variables):
            total = [None] * instances
            for k in range(1, (instances - 1) // 2 + 1):
                total[2 * k - 1] = float(k) * update[v][2 * k]
                total[2 * k] = -float(k) * update[v][2 * k - 1]
            for w in range(variables):
                if w != v:
                    entry = matrix(v, w)
                    for m in range(instances):
                        term = entry * update[w][m]
                        total[m] = term if total[m] is None else total[m] + term
            later.append([first[v][m] - scale[v] * total[m] for m in range(instances)])
        update = later
    solved = [from_harmonics(modes) for modes in update]
    return [[solved[v][i] for v in range(variables)] for i in range(instances)]


def base_kernel(state, source, matrix, axial_ghost, span_ghost, partial):
    instances, variables, _, circ, axial, span = state.shape
    _, _, _, _, axial_place, span_place = places()
    row = lax.broadcasted_iota(jnp.int32, (axial, span), 0)
    column = lax.broadcasted_iota(jnp.int32, (axial, span), 1)
    axial_row = jnp.where(axial_place == 0, axial - 1, 0)
    span_column = jnp.where(span_place == 0, span - 1, 0)
    columns = span_ghost[...]

    @pl.loop(0, circ * variables)
    def _(step):
        c = step // variables
        v = step % variables
        own = [state[i, v, 0, c] for i in range(instances)]
        timed = spectral_mix(own)
        for i in range(instances):
            k = (c * instances + i) * variables + v
            near = state[i, v, 0, 1 - c]
            near = near + jnp.where(row == 0, 0.0, pltpu.roll(own[i], 1, 0))
            near = near + jnp.where(row == axial - 1, 0.0, pltpu.roll(own[i], axial - 1, 0))
            near = near + jnp.where(row == axial_row, axial_ghost[pl.ds(k, 1), :], 0.0)
            near = near + jnp.where(column == 0, 0.0, pltpu.roll(own[i], 1, 1))
            near = near + jnp.where(column == span - 1, 0.0, pltpu.roll(own[i], span - 1, 1))
            edge = take_lanes(columns, jnp.full((axial, LANES), k, jnp.int32))
            edge = jnp.concatenate([edge] * (span // LANES), axis=1)
            near = near + jnp.where(column == span_column, edge, 0.0)
            local = matrix[v, 0, 0, c] * state[i, 0, 0, c]
            for w in range(1, variables):
                local = local + matrix[v, w, 0, c] * state[i, w, 0, c]
            partial[i, v, c] = source[i, v, 0, c] - (local - near + timed[i])


def finish_tile(c, t, right, state, matrix, residual, updated, buffers, sems):
    instances, variables = state.shape[:2]
    lanes = slice(t * LANES, (t + 1) * LANES)
    copies = [
        pltpu.make_async_copy(buffers.at[0], residual.at[:, :, 0, c, :, lanes], sems.at[0])
    ]
    cut = variables // 2
    for n, part in enumerate((slice(0, cut), slice(cut, variables)), 1):
        copies.append(
            pltpu.make_async_copy(
                buffers.at[1, :, part], updated.at[:, part, 0, c, :, lanes], sems.at[n]
            )
        )
    values = []
    for i in range(instances):
        values.append([])
        for v in range(variables):
            value = right(i, v, lanes)
            buffers[0, i, v] = value
            values[i].append(value)
    copies[0].start()
    update = solve_tile(values, lambda v, w: matrix[v, w, 0, c, :, lanes], (instances, variables))
    for v in range(variables):
        for i in range(instances):
            buffers[1, i, v] = state[i, v, 0, c, :, lanes] + update[i][v]
        if v == cut - 1:
            copies[1].start()
    copies[2].start()
    return copies


def near_kernel(partial, state, matrix, ghost, residual, updated, buffers, sems):
    near = places()[0]
    copies = []
    for t in range(partial.shape[-1] // LANES):
        copies += finish_tile(
            near,
            t,
            lambda i, v, lanes: partial[i, v, near, :, lanes] + ghost[i, v, :, lanes],
            state,
            matrix,
            residual,
            updated,
            buffers.at[t],
            sems.at[t],
        )
    for copy in copies:
        copy.wait()


def far_kernel(t, partial, state, matrix, middle, paired, _, __, residual, updated, buffers, sems):
    _, far, first, last, _, _ = places()

    def right(i, v, lanes):
        ghost = jnp.where(first | last, paired[i, v], middle[i, v, :, lanes])
        return partial[i, v, far, :, lanes] + ghost

    copies = finish_tile(far, t, right, state, matrix, residual, updated, buffers, sems)
    for copy in copies:
        copy.wait()


def call(kernel, name, operands, outs, ins, out_kinds=None, scratch=(), aliases=None):
    vmem = pl.BlockSpec(memory_space=pltpu.VMEM)
    anywhere = pl.BlockSpec(memory_space=pl.ANY)
    smem = pl.BlockSpec(memory_space=pltpu.SMEM)
    kinds = {"v": vmem, "a": anywhere, "s": smem}
    return pl.pallas_call(
        kernel,
        name=name,
        in_specs=[kinds[k] for k in ins],
        out_specs=[kinds[k] for k in out_kinds or "v" * len(outs)],
        out_shape=outs,
        scratch_shapes=scratch,
        input_output_aliases=aliases or {},
        compiler_params=pltpu.CompilerParams(vmem_limit_bytes=VMEM_LIMIT),
    )(*operands)


def shards(state, source, block_matrix, phase_index, face_pair):
    instances, variables, _, circ, axial, span = state.shape
    tiles = span // LANES
    blocks = lax.axis_size("blocks")
    cores = lax.axis_size("span")
    rings = blocks // AXB

    def array(*shape):
        return jax.ShapeDtypeStruct(shape, jnp.float32)

    def ring_partner(block, first):
        hop = 1 if block // AXB % 2 == first else -1
        return (block // AXB + hop) % rings * AXB + block % AXB

    def far_route(ends):
        route = []
        for block in range(blocks):
            for core in range(cores):
                if (block // AXB in (0, rings - 1)) == ends:
                    target = ring_partner(block, 1) * cores + core
                else:
                    target = block * cores + (core ^ 1)
                route.append((block * cores + core, target))
        return route

    both = ("blocks", "span")
    near_route = [(b, ring_partner(b, 0)) for b in range(blocks)]
    axial_route = [(b, b ^ 1) for b in range(blocks)]

    layer = array(instances, variables, axial, span)
    (near_face,) = call(
        functools.partial(layer_kernel, 0), "near_layer", (state,), [layer], "v"
    )
    near_ghost = lax.ppermute(near_face, "blocks", near_route)
    (far_face,) = call(
        functools.partial(layer_kernel, 1), "far_layer", (state, near_face), [layer], "va"
    )
    middle_ghost = lax.ppermute(far_face, both, far_route(False))

    faces = circ * instances * variables
    axial_face, span_face = call(
        faces_kernel,
        "faces",
        (state, far_face),
        [array(faces, span), array(axial, LANES)],
        "va",
    )
    axial_ghost = lax.ppermute(axial_face, "blocks", axial_route)
    span_ghost = lax.ppermute(span_face, "span", [(0, 1), (1, 0)])

    plus, minus = rotations(phase_index, instances)
    turn = jnp.where(lax.axis_index("blocks") < AXB, plus, minus)
    turn = jnp.broadcast_to(turn[:, None], (instances, LANES))
    chunks = [array(instances, variables, axial, LANES)] * tiles
    paired_faces = call(
        paired_kernel,
        "paired",
        (turn, face_pair.reshape(axial, span), state, span_face),
        chunks,
        "vvva",
        scratch=[pltpu.VMEM((tiles, axial, LANES), jnp.int32)],
    )
    paired_ghosts = [lax.ppermute(face, both, far_route(True)) for face in paired_faces]

    (partial,) = call(
        base_kernel,
        "base",
        (state, source, block_matrix, axial_ghost, span_ghost),
        [array(instances, variables, circ, axial, span)],
        "vvvvv",
    )
    out = array(*state.shape)
    tile = (2, instances, variables, axial, LANES)
    residual, updated = call(
        near_kernel,
        "near",
        (partial, state, block_matrix, near_ghost),
        [out, out],
        "vvvv",
        "aa",
        [pltpu.VMEM((tiles,) + tile, jnp.float32), pltpu.SemaphoreType.DMA((tiles, 3))],
    )
    for t, ghost in enumerate(paired_ghosts):
        residual, updated = call(
            functools.partial(far_kernel, t),
            "far",
            (partial, state, block_matrix, middle_ghost, ghost, residual, updated),
            [out, out],
            "vvvvvaa",
            "aa",
            [pltpu.VMEM(tile, jnp.float32), pltpu.SemaphoreType.DMA((3,))],
            {5: 0, 6: 1},
        )
    return updated, residual


def solution(mesh):
    placed = P(None, None, ("groups", "blocks"), None, None, "span")
    return jax.shard_map(
        shards,
        mesh=mesh,
        in_specs=(placed, placed, placed, P("groups"), P()),
        out_specs=(placed, placed),
        check_vma=False,
    )
```
